32 devices in a mesh: row: 2 (over y), col: 16 (over z, x, core).
Axes of the slice: x: 2, y: 2, z: 4, core: 2. Of those that a mesh axis runs over, the one named last changes fastest.
Arguments:
- features: bfloat16 [32768, 256], P('col', 'row'), may hold values from -6 to 6
- block_values: bfloat16 [2, 16, 256, 128, 128], P('row', 'col'), may hold values from -0.09375 to 0.09375
- block_coords: int32 [2, 16, 2, 256], P('row', 'col'), may hold values from 0 to 127, as said below
- live_blocks: int32 [2, 16], P('row', 'col'), may hold values from 32 to 256, as said below
- weight: bfloat16 [256, 256], replicated, may hold values from -0.375 to 0.375
- bias: float32 [256], replicated, may hold values from -3 to 3
- cotangent: bfloat16 [32768, 256], P(('row', 'col')), may hold values from -6 to 6
Outputs:
- out: bfloat16 [32768, 256], P(('row', 'col'))
- grad_x: bfloat16 [32768, 256], P('col', 'row')
- grad_weight: float32 [256, 256], replicated
- grad_bias: float32 [256], replicated
The draws below stay inside these ranges and needn't reach their ends.
Inputs may be any that keep to these rules, and one draw needn't show every extreme that they name: `block_coords`: within one tile the 256 slots name distinct pairs of a row block (0 to 127) and a column block (0 to 15). Only the first live_blocks[i, j] slots of tile (i, j) belong to the adjacency; some tile has all 256 slots live.
All inputs are finite; a program needn't handle non-finite values.
Results may differ from the reference program's by a relative error of at most 0.0075.
Values may be sent and summed in bfloat16 or wider, within the bound.
No kernel may reach another device: no remote copies, remote signals or barrier semaphores. Data moves between devices by JAX's collectives and lax.ppermute only.
A program may use at most 128 MiB of HBM per device.

```python
import jax
import jax.numpy as jnp
from jax import lax

F = 256
BS = 128
CB = 16
NB = 256
RB = 128
NODES = 32768
N_ROW = 2
N_COL = 16


def draw_live_blocks(key, part):
    first_key, second_key, third_key = jax.random.split(jax.random.fold_in(key, 11), 3)
    tiles_total = N_ROW * N_COL
    base_counts = jax.random.randint(first_key, (tiles_total,), NB // 8, NB // 2 + 1)
    heavy_tiles = jax.random.randint(second_key, (tiles_total,), 0, 8) == 0
    counts = jnp.where(heavy_tiles, NB, base_counts)
    chosen_tile = jax.random.randint(third_key, (), 0, tiles_total)
    counts = jnp.where(jnp.arange(tiles_total) == chosen_tile, NB, counts)
    return counts.reshape(N_ROW, N_COL).astype(jnp.int32)


def draw_block_coords(key, part):
    tiles_total = N_ROW * N_COL
    positions = RB * CB
    tile_keys = jax.random.split(jax.random.fold_in(key, 23), tiles_total)

    def one_tile(tile_key, tile_number):
        perm_key, slot_key = jax.random.split(tile_key)
        ordering = jax.random.permutation(perm_key, positions)
        target_slot = jax.random.randint(slot_key, (), 0, NB)
        last_place = jnp.argmax(ordering == positions - 1)
        moved = ordering.at[last_place].set(ordering[target_slot]).at[target_slot].set(positions - 1)
        ordering = jnp.where(tile_number == 0, moved, ordering)
        chosen = ordering[:NB]
        return jnp.stack([chosen // CB, chosen % CB])
    coords = jax.vmap(one_tile)(tile_keys, jnp.arange(tiles_total))
    return coords.reshape(N_ROW, N_COL, 2, NB).astype(jnp.int32)


def shard_levels(rng, dims, cuts, least, top_value):
    factor_of = 1.0
    for axis_at, parts in cuts:
        draws = jax.random.uniform(jax.random.fold_in(jax.random.fold_in(rng, 6), axis_at), (parts,), jnp.float32, least / len(cuts), top_value / len(cuts))
        factor_of = factor_of * jnp.repeat(jnp.exp(draws), dims[axis_at] // parts).reshape((-1,) + (1,) * (len(dims) - 1 - axis_at))
    return factor_of


def scatter_about(rng, extent, width, most, pieces=(), kind=jnp.bfloat16):
    entries = width * jax.random.normal(rng, extent, jnp.float32)
    if pieces:
        entries = entries * shard_levels(rng, extent, pieces, -0.22, 0.18)
    return jnp.clip(entries, -most, most).astype(kind)


def setup_inputs(seed: int = 0) -> dict:
    splits = jax.random.split(jax.random.key(seed), 8)
    features = scatter_about(splits[0], (NODES, F), 1.0, 6.0, ((0, 16), (1, 2)))
    block_values = scatter_about(splits[1], (N_ROW, N_COL, NB, BS, BS), (BS * NB * N_COL // RB) ** -0.5, 0.09375, ((0, 2), (1, 16)))
    block_coords = draw_block_coords(jax.random.fold_in(splits[7], 71), 0)
    live_blocks = draw_live_blocks(jax.random.fold_in(splits[7], 71), 0)
    weight = scatter_about(splits[4], (F, F), F ** -0.5, 0.375)
    bias = scatter_about(splits[5], (F,), 0.5, 3.0, (), jnp.float32)
    cotangent = scatter_about(splits[6], (NODES, F), 1.0, 6.0, ((0, 32),))
    return dict(features=features, block_values=block_values, block_coords=block_coords, live_blocks=live_blocks, weight=weight, bias=bias, cotangent=cotangent)


def reference(features, block_values, block_coords, live_blocks, weight, bias, cotangent):
    slot_ids = jnp.arange(NB, dtype=jnp.int32)
    feat_blocks = features.reshape(N_COL, CB, BS, F)

    def forward_row(row_idx):
        def one_tile(totals, col_idx):
            block_vals = block_values[row_idx, col_idx]
            row_ids = block_coords[row_idx, col_idx, 0]
            col_ids = block_coords[row_idx, col_idx, 1]
            alive_mask = slot_ids < live_blocks[row_idx, col_idx]
            picked = jnp.take(feat_blocks[col_idx], col_ids, axis=0)
            products = jnp.einsum('sab,sbf->saf', block_vals.astype(jnp.float32), picked.astype(jnp.float32))
            products = jnp.where(alive_mask[:, None, None], products, 0.0)
            return totals.at[row_ids].add(products), None

        totals, _ = lax.scan(one_tile, jnp.zeros((RB, BS, F), jnp.float32), jnp.arange(N_COL, dtype=jnp.int32))
        return totals

    aggregate = lax.map(forward_row, jnp.arange(N_ROW, dtype=jnp.int32)).reshape(NODES, F).astype(jnp.bfloat16)
    preact = jnp.dot(aggregate, weight, preferred_element_type=jnp.float32) + bias
    sigmoid_v = jax.nn.sigmoid(preact)
    out = (preact * sigmoid_v).astype(jnp.bfloat16)
    derivative = sigmoid_v * (1.0 + preact * (1.0 - sigmoid_v))
    grad_pre = (cotangent.astype(jnp.float32) * derivative).astype(jnp.bfloat16)
    norm_factor = NODES ** -0.5
    grad_weight = jnp.dot(aggregate.T, grad_pre, preferred_element_type=jnp.float32) * norm_factor
    grad_bias = jnp.sum(grad_pre.astype(jnp.float32), axis=0) * norm_factor
    grad_agg = jnp.dot(grad_pre, weight.T, preferred_element_type=jnp.float32).astype(jnp.bfloat16)
    grad_blocks = grad_agg.reshape(N_ROW, RB, BS, F)

    def backward_col(col_idx):
        def one_tile(totals, row_idx):
            block_vals = block_values[row_idx, col_idx]
            row_ids = block_coords[row_idx, col_idx, 0]
            col_ids = block_coords[row_idx, col_idx, 1]
            alive_mask = slot_ids < live_blocks[row_idx, col_idx]
            picked = jnp.take(grad_blocks[row_idx], row_ids, axis=0)
            products = jnp.einsum('sab,saf->sbf', block_vals.astype(jnp.float32), picked.astype(jnp.float32))
            products = jnp.where(alive_mask[:, None, None], products, 0.0)
            return totals.at[col_ids].add(products), None

        totals, _ = lax.scan(one_tile, jnp.zeros((CB, BS, F), jnp.float32), jnp.arange(N_ROW, dtype=jnp.int32))
        return totals

    grad_x = lax.map(backward_col, jnp.arange(N_COL, dtype=jnp.int32)).reshape(NODES, F).astype(jnp.bfloat16)
    return (out, grad_x, grad_weight, grad_bias)
```

```python
import functools

import jax
import jax.numpy as jnp
from jax import lax
from jax.experimental import pallas as pl
from jax.experimental.pallas import tpu as pltpu
from jax.sharding import PartitionSpec as P

BF16 = jnp.bfloat16
F32 = jnp.float32
GROUP = 32
VMEM_LIMIT = 56 * 1024 * 1024


def forward_kernel(live, dst, src, vals, feats, keep, send, totals):
    turn = pl.program_id(0)
    half = keep.shape[0]

    @pl.when(turn == 0)
    def _():
        def clear(at, _):
            totals[at] = jnp.zeros(totals.shape[1:], F32)
            return 0

        lax.fori_loop(0, totals.shape[0], clear, 0)

    @pl.when(turn * GROUP < live[0])
    def _():
        for u in range(GROUP):
            slot = turn * GROUP + u
            to = dst[slot]
            totals[to] += jnp.dot(vals[u], feats[src[slot]], preferred_element_type=F32)

    @pl.when(turn == pl.num_programs(0) - 1)
    def _():
        def write(at, _):
            keep[at] = totals[at].astype(BF16)
            send[at] = totals[half + at].astype(BF16)
            return 0

        lax.fori_loop(0, half, write, 0)


def forward_blocks(live, dst, src, vals, feats, rows):
    slots, size = vals.shape[0], vals.shape[1]
    width = feats.shape[2]
    half = rows // 2
    last = lambda live: jnp.maximum((live[0] + GROUP - 1) // GROUP - 1, 0)
    whole = lambda shape: pl.BlockSpec(shape, lambda t, *_: (0,) * len(shape))
    part = jax.ShapeDtypeStruct((half, size, width), BF16)
    return pl.pallas_call(
        forward_kernel,
        grid_spec=pltpu.PrefetchScalarGridSpec(
            num_scalar_prefetch=3,
            grid=(slots // GROUP,),
            in_specs=[
                pl.BlockSpec((GROUP, size, size), lambda t, live, *_: (jnp.minimum(t, last(live)), 0, 0)),
                whole(feats.shape),
            ],
            out_specs=[whole(part.shape), whole(part.shape)],
            scratch_shapes=[pltpu.VMEM((rows + 1, size, width), F32)],
        ),
        out_shape=[part, part],
        compiler_params=pltpu.CompilerParams(vmem_limit_bytes=VMEM_LIMIT),
        cost_estimate=pl.CostEstimate(
            flops=8 * slots * size * size * width, bytes_accessed=4 * vals.size, transcendentals=0
        ),
        name="forward_blocks",
    )(live, dst, src, vals, feats)


def backward_kernel(live, dst, src, vals, grads, out, totals):
    turn = pl.program_id(0)

    @pl.when(turn == 0)
    def _():
        def clear(at, _):
            totals[at] = jnp.zeros(totals.shape[1:], F32)
            return 0

        lax.fori_loop(0, totals.shape[0], clear, 0)

    @pl.when(turn * GROUP < live[0])
    def _():
        for u in range(GROUP):
            slot = turn * GROUP + u
            to = dst[slot]
            totals[to] += jnp.dot(grads[src[slot]], vals[u], preferred_element_type=F32)

    @pl.when(turn == pl.num_programs(0) - 1)
    def _():
        def write(at, _):
            out[at] = totals[at].T.astype(out.dtype)
            return 0

        lax.fori_loop(0, out.shape[0], write, 0)


def backward_blocks(live, dst, src, vals, grads, cols, kind):
    slots, size = vals.shape[0], vals.shape[1]
    width = grads.shape[1]
    last = lambda live: jnp.maximum((live[0] + GROUP - 1) // GROUP - 1, 0)
    whole = lambda shape: pl.BlockSpec(shape, lambda t, *_: (0,) * len(shape))
    result = jax.ShapeDtypeStruct((cols, size, width), kind)
    return pl.pallas_call(
        backward_kernel,
        grid_spec=pltpu.PrefetchScalarGridSpec(
            num_scalar_prefetch=3,
            grid=(slots // GROUP,),
            in_specs=[
                pl.BlockSpec((GROUP, size, size), lambda t, live, *_: (jnp.minimum(t, last(live)), 0, 0)),
                whole(grads.shape),
            ],
            out_specs=whole(result.shape),
            scratch_shapes=[pltpu.VMEM((cols + 1, width, size), F32)],
        ),
        out_shape=result,
        compiler_params=pltpu.CompilerParams(vmem_limit_bytes=VMEM_LIMIT),
        cost_estimate=pl.CostEstimate(
            flops=8 * slots * size * size * width, bytes_accessed=4 * vals.size, transcendentals=0
        ),
        name="backward_blocks",
    )(live, dst, src, vals, grads)


def dense_kernel(
    first, keep_a, got_a, keep_b, got_b, cot, weight, bias, out, grad_a, grad_b, terms
):
    half = keep_a.shape[1]
    size = grad_a.shape[2]
    at_a = pl.multiple_of(first[0] * half, half)
    at_b = pl.multiple_of((1 - first[0]) * half, half)
    total = lambda x, y: (x[...].astype(F32) + y[...].astype(F32)).astype(BF16)
    agg_a, agg_b = total(keep_a, got_a), total(keep_b, got_b)
    weight_a, weight_b = weight[pl.ds(at_a, half), :], weight[pl.ds(at_b, half), :]
    preact = jnp.dot(agg_a, weight_a, preferred_element_type=F32)
    preact += jnp.dot(agg_b, weight_b, preferred_element_type=F32)
    preact += bias[...]
    gate = jax.nn.sigmoid(preact)
    out[...] = (preact * gate).astype(BF16)
    slope = gate * (1.0 + preact * (1.0 - gate))
    grad_pre = (cot[...].astype(F32) * slope).astype(BF16)
    over_rows = (((0,), (0,)), ((), ()))
    over_outputs = (((1,), (1,)), ((), ()))
    terms[pl.ds(at_a, half), :] = lax.dot_general(agg_a, grad_pre, over_rows, preferred_element_type=F32)
    terms[pl.ds(at_b, half), :] = lax.dot_general(agg_b, grad_pre, over_rows, preferred_element_type=F32)
    sums = jnp.sum(grad_pre.astype(F32), axis=0, keepdims=True)
    terms[2 * half :, :] = jnp.broadcast_to(sums, (terms.shape[0] - 2 * half, sums.shape[1]))
    turned_a = lax.dot_general(weight_a, grad_pre, over_outputs, preferred_element_type=F32).astype(BF16)
    turned_b = lax.dot_general(weight_b, grad_pre, over_outputs, preferred_element_type=F32).astype(BF16)
    for at in range(grad_a.shape[0]):
        grad_a[at] = turned_a[:, at * size : (at + 1) * size]
        grad_b[at] = turned_b[:, at * size : (at + 1) * size]


def dense(first, keep_a, got_a, keep_b, got_b, cot, weight, bias, size):
    rows, half = keep_a.shape
    width = cot.shape[1]
    vmem = pl.BlockSpec(memory_space=pltpu.VMEM)
    turned = jax.ShapeDtypeStruct((rows // size, half, size), BF16)
    return pl.pallas_call(
        dense_kernel,
        in_specs=[pl.BlockSpec(memory_space=pltpu.SMEM)] + [vmem] * 7,
        out_specs=[vmem] * 4,
        out_shape=[
            jax.ShapeDtypeStruct((rows, width), BF16),
            turned,
            turned,
            jax.ShapeDtypeStruct((2 * half + 8, width), F32),
        ],
        compiler_params=pltpu.CompilerParams(vmem_limit_bytes=VMEM_LIMIT),
        cost_estimate=pl.CostEstimate(
            flops=8 * rows * width * width, bytes_accessed=8 * rows * width, transcendentals=rows * width
        ),
        name="dense_layer",
    )(first, keep_a, got_a, keep_b, got_b, cot, weight, bias)


def swap(array, axis, bit):
    return lax.ppermute(array, axis, [(at, at ^ bit) for at in range(lax.axis_size(axis))])


def add(x, y):
    return (x.astype(F32) + y.astype(F32)).astype(BF16)


def scatter_sum(keep, send):
    count = lax.axis_size("col")
    bit = 1
    while True:
        got = swap(send, "col", bit)
        bit *= 2
        if bit == count:
            return keep, got
        half = keep.shape[0] // 2
        keep, send = add(keep[:half], got[:half]), add(keep[half:], got[half:])


def gather(part):
    bit = lax.axis_size("col") // 2
    while bit:
        part = jnp.concatenate([part, swap(part, "col", bit)], axis=0)
        bit //= 2
    return part


def on_device(features, block_values, block_coords, live_blocks, weight, bias, cotangent):
    vals = block_values[0, 0]
    size = vals.shape[1]
    live = live_blocks[0]
    row_count, col_count = lax.axis_size("row"), lax.axis_size("col")
    me = lax.axis_index("col")
    width = weight.shape[0]
    half = width // 2
    per_device = cotangent.shape[0] // size
    rows = per_device * col_count
    cols = features.shape[0] // size

    row_ids, col_ids = block_coords[0, 0, 0], block_coords[0, 0, 1]
    owner = (row_ids // per_device) ^ me
    place = jnp.zeros_like(owner)
    bit, turned = 1, col_count // 2
    while bit < col_count:
        place = place + jnp.where((owner & bit) != 0, turned, 0)
        bit, turned = bit * 2, turned // 2
    row_place = place * per_device + row_ids % per_device
    alive = jnp.arange(vals.shape[0], dtype=jnp.int32) < live[0]
    row_dst = jnp.where(alive, row_place, rows)
    col_dst = jnp.where(alive, col_ids, cols)

    if row_count == 2:
        first = lax.axis_index("row").reshape(1)
        feats_a, feats_b = features, swap(features, "row", 1)
    else:
        first = jnp.zeros((1,), jnp.int32)
        feats = lax.all_gather(features, "row", axis=1, tiled=True)
        feats_a, feats_b = feats[:, :half], feats[:, half:]

    def aggregate_terms(feats):
        keep, send = forward_blocks(live, row_dst, col_ids, vals, feats.reshape(cols, size, half), rows)
        keep, got = scatter_sum(keep, send)
        return keep.reshape(-1, half), got.reshape(-1, half)

    keep_a, got_a = aggregate_terms(feats_a)
    keep_b, got_b = aggregate_terms(feats_b)
    out, grad_a, grad_b, terms = dense(
        first, keep_a, got_a, keep_b, got_b, cotangent, weight, bias.reshape(1, -1), size
    )
    sums = lax.psum(terms, ("row", "col")) * (cols * size * col_count) ** (-0.5)

    def input_grad(grad, kind):
        return backward_blocks(live, col_dst, row_place, vals, gather(grad), cols, kind).reshape(-1, half)

    if row_count == 2:
        theirs = swap(input_grad(grad_b, BF16), "row", 1)
        grad_x = (input_grad(grad_a, F32) + theirs.astype(F32)).astype(BF16)
    else:
        partial_x = jnp.concatenate([input_grad(grad_a, F32), input_grad(grad_b, F32)], axis=1)
        grad_x = lax.psum_scatter(partial_x, "row", scatter_dimension=1, tiled=True).astype(BF16)
    return out, grad_x, sums[:width], sums[width]


def solution(mesh):
    in_specs = (
        P("col", "row"),
        P("row", "col", None, None, None),
        P("row", "col", None, None),
        P("row", "col"),
        P(),
        P(),
        P(("row", "col"), None),
    )
    out_specs = (P(("row", "col"), None), P("col", "row"), P(), P())
    return jax.shard_map(
        on_device, mesh=mesh, in_specs=in_specs, out_specs=out_specs, check_vma=False
    )
```

```python
import functools

import jax
import jax.numpy as jnp
from jax import lax
from jax.experimental import pallas as pl
from jax.experimental.pallas import tpu as pltpu
from jax.sharding import PartitionSpec as P

BF16 = jnp.bfloat16
F32 = jnp.float32
GROUP = 32
PARTS = 2
VMEM_LIMIT = 56 * 1024 * 1024


def orders(count):
    bits = [1 << k for k in range(count.bit_length() - 1)]
    swapped = list(bits)
    swapped[1], swapped[2] = bits[2], bits[1]
    return bits, swapped


def spot_of(apart, order):
    spot = apart * 0
    for k, bit in enumerate(reversed(order)):
        spot = spot + jnp.where((apart & bit) != 0, 1 << k, 0)
    return spot


def split_row(row, me, count, per_device, parts):
    run = per_device // parts
    apart, at = (row // per_device) ^ me, row % per_device
    spots = [spot_of(apart, order) for order in orders(count)[:parts]]
    part = at // run
    spot = spots[0] if parts == 1 else jnp.where(part == 0, spots[0], spots[1])
    return spot, part, at % run


def prepare(live, totals, spots, index_of, clear_count):
    each = spots.shape[0] // clear_count

    def one(at, _):
        totals[at] = jnp.zeros(totals.shape[1:], F32)
        for k in range(each):
            slot = at * each + k
            spots[slot] = index_of(slot, slot < live[0])
        return 0

    lax.fori_loop(0, clear_count, one, 0)


def block_copies(vals, held, sems):
    groups = held.shape[0] // GROUP
    part = lambda at: pl.ds(at * GROUP, GROUP)
    return [pltpu.make_async_copy(vals.at[part(at)], held.at[part(at)], sems.at[at]) for at in range(groups)]


def over_blocks(live, copies, body):
    for at, copy in enumerate(copies):

        @pl.when(at * GROUP < live[0])
        def _(at=at, copy=copy):
            copy.wait()
            for u in range(GROUP):
                body(at * GROUP + u)


def start_blocks(live, copies):
    for at, copy in enumerate(copies):

        @pl.when(at * GROUP < live[0])
        def _(copy=copy):
            copy.start()


def forward_kernel(count, per_device, live, me, coords, vals, feats, keep, send, held, totals, rounded, spots, sems, out_sems):
    rows = count * per_device
    half, run, below = rows // 2, per_device // PARTS, count // 2
    copies = block_copies(vals, held, sems)
    start_blocks(live, copies)

    def index_of(slot, alive):
        spot, part, at = split_row(coords[0, slot], me[0], count, per_device, PARTS)
        to = (((spot // below) * PARTS + part) * below + spot % below) * run + at
        return jnp.where(alive, to, rows)

    prepare(live, totals, spots, index_of, rows)

    def one_slot(slot):
        to = spots[slot]
        totals[to] += jnp.dot(held[slot], feats[coords[1, slot]], preferred_element_type=F32)

    over_blocks(live, copies, one_slot)
    outs = []
    for at, out in ((1, send), (0, keep)):

        def write(k, _, at=at):
            rounded[at * half + k] = totals[at * half + k].astype(BF16)
            return 0

        lax.fori_loop(0, half, write, 0)
        outs.append(pltpu.make_async_copy(rounded.at[pl.ds(at * half, half)], out, out_sems.at[at]))
        outs[-1].start()
    for out in outs:
        out.wait()


def forward_blocks(live, me, coords, vals, feats, count, per_device):
    slots, size = vals.shape[0], vals.shape[1]
    width = feats.shape[2]
    rows = count * per_device
    part = jax.ShapeDtypeStruct((rows // 2, size, width), BF16)
    smem, hbm = pl.BlockSpec(memory_space=pltpu.SMEM), pl.BlockSpec(memory_space=pl.ANY)
    return pl.pallas_call(
        functools.partial(forward_kernel, count, per_device),
        in_specs=[smem, smem, smem, hbm, pl.BlockSpec(memory_space=pltpu.VMEM)],
        out_specs=[hbm, hbm],
        scratch_shapes=[
            pltpu.VMEM(vals.shape, BF16),
            pltpu.VMEM((rows + 1, size, width), F32),
            pltpu.VMEM((rows, size, width), BF16),
            pltpu.SMEM((slots,), jnp.int32),
            pltpu.SemaphoreType.DMA((slots // GROUP,)),
            pltpu.SemaphoreType.DMA((2,)),
        ],
        out_shape=[part, part],
        compiler_params=pltpu.CompilerParams(vmem_limit_bytes=VMEM_LIMIT),
        cost_estimate=pl.CostEstimate(
            flops=8 * slots * size * size * width, bytes_accessed=4 * vals.size, transcendentals=0
        ),
        name="forward_blocks",
    )(live, me, coords, vals, feats)


def backward_kernel(count, per_device, parts, lengths, live, me, coords, vals, *refs):
    pieces, (out, held, grads, totals, spots, sems, piece_sems) = refs[:-7], refs[-7:]
    run, cols = per_device // parts, out.shape[0]
    copies = block_copies(vals, held, sems)
    fetches, start = [], 0
    for at, (piece, length) in enumerate(zip(pieces, lengths)):
        fetches.append(pltpu.make_async_copy(piece, grads.at[pl.ds(start, length)], piece_sems.at[at]))
        fetches[-1].start()
        start += length
    start_blocks(live, copies)

    def index_of(slot, alive):
        spot, part, at = split_row(coords[0, slot], me[0], count, per_device, parts)
        return (part * count + spot) * run + at

    prepare(live, totals, spots, index_of, cols)
    for fetch in fetches:
        fetch.wait()

    def one_slot(slot):
        to = jnp.where(slot < live[0], coords[1, slot], cols)
        totals[to] += jnp.dot(grads[spots[slot]], held[slot], preferred_element_type=F32)

    over_blocks(live, copies, one_slot)

    def write(at, _):
        out[at] = totals[at].T.astype(out.dtype)
        return 0

    lax.fori_loop(0, cols, write, 0)


def backward_blocks(live, me, coords, vals, pieces, cols, kind, count, per_device, parts):
    slots, size = vals.shape[0], vals.shape[1]
    width = pieces[0].shape[1]
    lengths = tuple(piece.shape[0] for piece in pieces)
    smem, hbm = pl.BlockSpec(memory_space=pltpu.SMEM), pl.BlockSpec(memory_space=pl.ANY)
    return pl.pallas_call(
        functools.partial(backward_kernel, count, per_device, parts, lengths),
        in_specs=[smem, smem, smem, hbm] + [hbm] * len(pieces),
        out_specs=pl.BlockSpec(memory_space=pltpu.VMEM),
        scratch_shapes=[
            pltpu.VMEM(vals.shape, BF16),
            pltpu.VMEM((count * per_device, width, size), BF16),
            pltpu.VMEM((cols + 1, width, size), F32),
            pltpu.SMEM((slots,), jnp.int32),
            pltpu.SemaphoreType.DMA((slots // GROUP,)),
            pltpu.SemaphoreType.DMA((len(pieces),)),
        ],
        out_shape=jax.ShapeDtypeStruct((cols, size, width), kind),
        compiler_params=pltpu.CompilerParams(vmem_limit_bytes=VMEM_LIMIT),
        cost_estimate=pl.CostEstimate(
            flops=8 * slots * size * size * width, bytes_accessed=4 * vals.size, transcendentals=0
        ),
        name="backward_blocks",
    )(live, me, coords, vals, *pieces)


def dense_kernel(first, *refs):
    terms_a, terms_b, (cot, weight, bias, out, grad_a, grad_b, terms) = refs[:4], refs[4:8], refs[8:]
    half = weight.shape[0] // 2
    size = grad_a.shape[2]
    at_a = pl.multiple_of(first[0] * half, half)
    at_b = pl.multiple_of((1 - first[0]) * half, half)

    def total(keep_0, got_0, keep_1, got_1):
        add_up = lambda x, y: (x[...].astype(F32) + y[...].astype(F32)).astype(BF16).reshape(-1, half)
        return jnp.concatenate([add_up(keep_0, got_0), add_up(keep_1, got_1)])

    agg_a, agg_b = total(*terms_a), total(*terms_b)
    weight_a, weight_b = weight[pl.ds(at_a, half), :], weight[pl.ds(at_b, half), :]
    preact = jnp.dot(agg_a, weight_a, preferred_element_type=F32)
    preact += jnp.dot(agg_b, weight_b, preferred_element_type=F32)
    preact += bias[...]
    gate = jax.nn.sigmoid(preact)
    out[...] = (preact * gate).astype(BF16)
    slope = gate * (1.0 + preact * (1.0 - gate))
    grad_pre = (cot[...].astype(F32) * slope).astype(BF16)
    over_rows = (((0,), (0,)), ((), ()))
    over_outputs = (((1,), (1,)), ((), ()))
    turned_a = lax.dot_general(weight_a, grad_pre, over_outputs, preferred_element_type=F32).astype(BF16)
    turned_b = lax.dot_general(weight_b, grad_pre, over_outputs, preferred_element_type=F32).astype(BF16)
    for at in range(grad_a.shape[0]):
        grad_a[at] = turned_a[:, at * size : (at + 1) * size]
        grad_b[at] = turned_b[:, at * size : (at + 1) * size]
    terms[pl.ds(at_a, half), :] = lax.dot_general(agg_a, grad_pre, over_rows, preferred_element_type=F32)
    terms[pl.ds(at_b, half), :] = lax.dot_general(agg_b, grad_pre, over_rows, preferred_element_type=F32)
    sums = jnp.sum(grad_pre.astype(F32), axis=0, keepdims=True)
    terms[2 * half :, :] = jnp.broadcast_to(sums, (terms.shape[0] - 2 * half, sums.shape[1]))


def dense(first, terms_a, terms_b, cot, weight, bias):
    run, size, half = terms_b[0].shape
    rows, width = cot.shape
    vmem = pl.BlockSpec(memory_space=pltpu.VMEM)
    turned = jax.ShapeDtypeStruct((rows // size, half, size), BF16)
    return pl.pallas_call(
        dense_kernel,
        in_specs=[pl.BlockSpec(memory_space=pltpu.SMEM)] + [vmem] * 11,
        out_specs=[vmem] * 4,
        out_shape=[
            jax.ShapeDtypeStruct((rows, width), BF16),
            turned,
            turned,
            jax.ShapeDtypeStruct((2 * half + 32, width), F32),
        ],
        compiler_params=pltpu.CompilerParams(vmem_limit_bytes=VMEM_LIMIT),
        cost_estimate=pl.CostEstimate(
            flops=8 * rows * width * width, bytes_accessed=8 * rows * width, transcendentals=rows * width
        ),
        name="dense_layer",
    )(first, *terms_a, *terms_b, cot, weight, bias)


def swap(array, axis, bit):
    return lax.ppermute(array, axis, [(at, at ^ bit) for at in range(lax.axis_size(axis))])


def after(array, *others):
    return lax.optimization_barrier((array, *others))[0]


def add(x, y):
    return (x.astype(F32) + y.astype(F32)).astype(BF16)


def halves(keep, got):
    half = keep.shape[0] // 2
    send = add(keep[half:], got[half:])
    return add(keep[:half], got[:half]), send


class SumOverAll:
    def __init__(self, terms):
        self.terms = self.got = terms
        self.bits = [1 << k for k in range(lax.axis_size("col").bit_length() - 1)]
        if lax.axis_size("row") == 2:
            half = terms.shape[0] // 2
            self.mine = lax.axis_index("row")
            self.part = lax.dynamic_slice_in_dim(terms, self.mine * half, half)
            self.got = swap(lax.dynamic_slice_in_dim(terms, (1 - self.mine) * half, half), "row", 1)

    def step(self, take=lambda got: got):
        if lax.axis_size("row") == 2 and self.bits:
            self.part = self.part + take(self.got)
            self.got = swap(self.part, "col", self.bits.pop(0))

    def finish(self):
        if lax.axis_size("row") != 2:
            return lax.psum(self.terms, ("row", "col"))
        while self.bits:
            self.step()
        part = self.part + self.got
        other = swap(part, "row", 1)
        first, second = jnp.where(self.mine == 0, part, other), jnp.where(self.mine == 0, other, part)
        return jnp.concatenate([first, second])


def on_device(features, block_values, block_coords, live_blocks, weight, bias, cotangent):
    vals, coords, live = block_values[0, 0], block_coords[0, 0], live_blocks[0]
    size = vals.shape[1]
    row_count, count = lax.axis_size("row"), lax.axis_size("col")
    me = lax.axis_index("col").reshape(1)
    width = weight.shape[0]
    half = width // 2
    per_device = cotangent.shape[0] // size
    cols = features.shape[0] // size
    order_0, order_1 = orders(count)

    if row_count == 2:
        first = lax.axis_index("row").reshape(1)
        feats_a, feats_b = features, swap(features, "row", 1)
    else:
        first = jnp.zeros((1,), jnp.int32)
        feats = lax.all_gather(features, "row", axis=1, tiled=True)
        feats_a, feats_b = feats[:, :half], feats[:, half:]

    def core_sums(feats, *others):
        keep, send = forward_blocks(live, me, coords, vals, feats.reshape(cols, size, half), count, per_device)
        got = swap(after(send, *others), "col", 1)
        part = keep.shape[0] // 2
        return halves(keep[:part], got[:part]), halves(keep[part:], got[part:])

    def next_step(part, bit):
        keep, send = part
        return halves(keep, swap(send, "col", bit))

    a0, a1 = core_sums(feats_a, feats_b)
    feats_b = after(feats_b, a0[1], a1[1])
    a0, a1 = next_step(a0, order_0[1]), next_step(a1, order_1[1])
    b0, b1 = core_sums(feats_b, a0[1], a1[1])
    for bit_0, bit_1 in zip(order_0[2:-1], order_1[2:-1]):
        a0, a1 = next_step(a0, bit_0), next_step(a1, bit_1)
    for bit_0, bit_1 in zip(order_0[1:-1], order_1[1:-1]):
        b0, b1 = next_step(b0, bit_0), next_step(b1, bit_1)
    terms_a, terms_b = [], []
    for terms, parts in ((terms_a, (a0, a1)), (terms_b, (b0, b1))):
        for keep, send in parts:
            terms += [keep, swap(send, "col", order_0[-1])]
    out, grad_a, grad_b, terms = dense(first, terms_a, terms_b, cotangent, weight, bias.reshape(1, -1))
    run = per_device // PARTS

    def input_grad(pieces, parts, kind):
        result = backward_blocks(live, me, coords, vals, pieces, cols, kind, count, per_device, parts)
        return result.reshape(-1, half)

    taken = [grad_b]

    def take(got):
        taken[0] = after(got, taken[0])
        return taken[0]

    totals = SumOverAll(terms)
    outer, inner = list(reversed(order_0[2:])), order_0[1]
    got_b = swap(grad_b, "col", outer[0])
    pieces_a = [grad_a]
    crossed = [swap(grad_a, "col", inner)]
    sent_a = {bit: swap(grad_a, "col", bit) for bit in outer[1:]}
    crossed = [take(crossed[0])]
    totals.step(take)
    got_b = take(got_b)
    parts_b = [jnp.concatenate([grad_b[at : at + run], got_b[at : at + run]]) for at in (0, run)]
    steps_b = list(zip(reversed(order_0[1:-1]), reversed(order_1[1:-1])))

    def step_b(at):
        got = [swap(part, "col", bit) for part, bit in zip(parts_b, steps_b[at])]
        return got

    for at in range(len(steps_b)):
        got = step_b(at)
        if at == 0:
            got_a = swap(after(grad_a, got_b), "col", outer[0])
        got = [take(part) for part in got]
        parts_b = [jnp.concatenate([part, more]) for part, more in zip(parts_b, got)]
        totals.step(take)
        if at == 0:
            got_a = take(got_a)
            pieces_a = [grad_a, got_a]
            for bit in outer[1:]:
                pieces_a = pieces_a + [sent_a[bit]] + [swap(piece, "col", bit) for piece in pieces_a[1:]]
            crossed += [swap(piece, "col", inner) for piece in pieces_a[1:]]
    core_b = [swap(part, "col", 1) for part in parts_b]
    early = jnp.concatenate(pieces_a + [take(piece) for piece in crossed[:-1]])
    pieces_b = [parts_b[0], core_b[0], parts_b[1], core_b[1]]
    totals.step(take)
    pieces_b[0] = after(pieces_b[0], taken[0])
    core_early = swap(early, "col", 1)

    if row_count == 2:
        part_b = input_grad(pieces_b, PARTS, BF16)
        theirs = swap(part_b, "row", 1)
        late = after(crossed[-1], part_b)
        pieces_a = [early, late, core_early, swap(late, "col", 1)]
        grad_x = (input_grad(pieces_a, 1, F32) + theirs.astype(F32)).astype(BF16)
    else:
        part_b = input_grad(pieces_b, PARTS, F32)
        pieces_a = [early, crossed[-1], core_early, swap(crossed[-1], "col", 1)]
        partial_x = jnp.concatenate([input_grad(pieces_a, 1, F32), part_b], axis=1)
        grad_x = lax.psum_scatter(partial_x, "row", scatter_dimension=1, tiled=True).astype(BF16)
    totals.got = after(totals.got, part_b)
    sums = totals.finish() * (cols * size * count) ** (-0.5)
    return out, grad_x, sums[:width], sums[width]


def solution(mesh):
    in_specs = (
        P("col", "row"),
        P("row", "col", None, None, None),
        P("row", "col", None, None),
        P("row", "col"),
        P(),
        P(),
        P(("row", "col"), None),
    )
    out_specs = (P(("row", "col"), None), P("col", "row"), P(), P())
    return jax.shard_map(
        on_device, mesh=mesh, in_specs=in_specs, out_specs=out_specs, check_vma=False
    )
```

```python
import functools
import math

import jax
import jax.numpy as jnp
from jax import lax
from jax.experimental import pallas as pl
from jax.experimental.pallas import tpu as pltpu
from jax.sharding import PartitionSpec as P

BF16 = jnp.bfloat16
F32 = jnp.float32
GROUP = 32
EARLY = 2
PARTS = 2
VMEM_LIMIT = 56 * 1024 * 1024


def orders(count):
    bits = [1 << k for k in range(count.bit_length() - 1)]
    swapped = list(bits)
    swapped[1], swapped[2] = bits[2], bits[1]
    return bits, swapped


def spot_of(apart, order):
    spot = apart * 0
    for k, bit in enumerate(reversed(order)):
        spot = spot + jnp.where((apart & bit) != 0, 1 << k, 0)
    return spot


def split_row(row, me, per_device, plan):
    run = per_device // len(plan)
    apart, at = (row // per_device) ^ me, row % per_device
    part = at // run
    spot = spot_of(apart, plan[0])
    for number, order in enumerate(plan[1:], 1):
        spot = jnp.where(part == number, spot_of(apart, order), spot)
    return spot, part, at % run


def clear(totals, count):
    steps = math.gcd(count, 16)
    height = count // steps

    def one(at, _):
        totals[pl.ds(at * height, height)] = jnp.zeros((height,) + totals.shape[1:], F32)
        return 0

    lax.fori_loop(0, steps, one, 0)


def start_table(sources, targets, table, scalars, sem):
    table[0:1, :] = sources
    table[1:2, :] = targets
    copy = pltpu.make_async_copy(table, scalars, sem)
    copy.start()
    return copy


def alive_slots(live, slots):
    return lax.broadcasted_iota(jnp.int32, (1, slots), 1) < live[0]


def block_copies(vals, held, sems):
    groups = held.shape[0] // GROUP
    part = lambda at: pl.ds(at * GROUP, GROUP)
    return [pltpu.make_async_copy(vals.at[part(at)], held.at[part(at)], sems.at[at]) for at in range(groups)]


def over_blocks(live, copies, body):
    for at, copy in enumerate(copies):

        @pl.when(at * GROUP < live[0])
        def _(at=at, copy=copy):
            copy.wait()
            for u in range(GROUP):
                body(at * GROUP + u)


def start_blocks(live, copies, first=0, last=None):
    for at, copy in list(enumerate(copies))[first:last]:

        @pl.when(at * GROUP < live[0])
        def _(copy=copy):
            copy.start()


def forward_kernel(
    plan, per_device, live, me, coords, vals, feats, keep, send, held, totals, rounded, table, scalars, sems, out_sems
):
    parts = len(plan)
    half, run = keep.shape[0], per_device // parts
    rows, below = 2 * half, half // per_device
    copies = block_copies(vals, held, sems)
    start_blocks(live, copies)
    spot, part, at = split_row(coords[0:1, :], me[0], per_device, plan)
    to = (((spot // below) * parts + part) * below + spot % below) * run + at
    to = jnp.where(alive_slots(live, to.shape[1]), to, rows)
    filled = start_table(coords[1:2, :], to, table, scalars, out_sems.at[0])
    clear(totals, rows)
    filled.wait()

    def one_slot(slot):
        to = scalars[1, slot]
        totals[to] += jnp.dot(held[slot], feats[scalars[0, slot]], preferred_element_type=F32)

    over_blocks(live, copies, one_slot)
    outs = []
    for at, out in ((1, send), (0, keep)):

        height = math.gcd(half, 8)

        def write(k, _, at=at):
            here = pl.ds(at * half + k * height, height)
            rounded[here] = totals[here].astype(BF16)
            return 0

        lax.fori_loop(0, half // height, write, 0)
        outs.append(pltpu.make_async_copy(rounded.at[pl.ds(at * half, half)], out, out_sems.at[at]))
        outs[-1].start()
    for out in outs:
        out.wait()


def forward_blocks(live, me, coords, vals, feats, plan, per_device):
    slots, size = vals.shape[0], vals.shape[1]
    width = feats.shape[2]
    rows = (1 << len(plan[0])) * per_device
    part = jax.ShapeDtypeStruct((rows // 2, size, width), BF16)
    smem, hbm = pl.BlockSpec(memory_space=pltpu.SMEM), pl.BlockSpec(memory_space=pl.ANY)
    vmem = pl.BlockSpec(memory_space=pltpu.VMEM)
    return pl.pallas_call(
        functools.partial(forward_kernel, plan, per_device),
        in_specs=[smem, smem, vmem, hbm, vmem],
        out_specs=[hbm, hbm],
        scratch_shapes=[
            pltpu.VMEM(vals.shape, BF16),
            pltpu.VMEM((rows + 1, size, width), F32),
            pltpu.VMEM((rows, size, width), BF16),
            pltpu.VMEM((2, slots), jnp.int32),
            pltpu.SMEM((2, slots), jnp.int32),
            pltpu.SemaphoreType.DMA((slots // GROUP,)),
            pltpu.SemaphoreType.DMA((2,)),
        ],
        out_shape=[part, part],
        compiler_params=pltpu.CompilerParams(vmem_limit_bytes=VMEM_LIMIT),
        cost_estimate=pl.CostEstimate(
            flops=8 * slots * size * size * width, bytes_accessed=4 * vals.size, transcendentals=0
        ),
        name="forward_blocks",
    )(live, me, coords, vals, feats)


def backward_kernel(plan, per_device, lengths, live, me, coords, vals, *refs):
    pieces, (out, held, grads, totals, table, scalars, sems, piece_sems) = refs[:-8], refs[-8:]
    run, cols, count = per_device // len(plan), out.shape[0], 1 << len(plan[0])
    copies = block_copies(vals, held, sems)
    fetches, start = [], 0
    for at, (piece, length) in enumerate(zip(pieces, lengths)):
        fetches.append(pltpu.make_async_copy(piece, grads.at[pl.ds(start, length)], piece_sems.at[at]))
        fetches[-1].start()
        start += length
    start_blocks(live, copies, last=EARLY)
    spot, part, at = split_row(coords[0:1, :], me[0], per_device, plan)
    alive = alive_slots(live, spot.shape[1])
    to = jnp.where(alive, coords[1:2, :], cols)
    filled = start_table((part * count + spot) * run + at, to, table, scalars, piece_sems.at[len(pieces)])
    clear(totals, cols)
    filled.wait()
    for fetch in fetches:
        fetch.wait()
    start_blocks(live, copies, first=EARLY)

    def one_slot(slot):
        to = scalars[1, slot]
        totals[to] += jnp.dot(grads[scalars[0, slot]], held[slot], preferred_element_type=F32)

    over_blocks(live, copies, one_slot)

    def write(at, _):
        out[at] = totals[at].T.astype(out.dtype)
        return 0

    lax.fori_loop(0, cols, write, 0)


def backward_blocks(live, me, coords, vals, pieces, cols, kind, plan, per_device):
    slots, size = vals.shape[0], vals.shape[1]
    width = pieces[0].shape[1]
    lengths = tuple(piece.shape[0] for piece in pieces)
    smem, hbm = pl.BlockSpec(memory_space=pltpu.SMEM), pl.BlockSpec(memory_space=pl.ANY)
    vmem = pl.BlockSpec(memory_space=pltpu.VMEM)
    return pl.pallas_call(
        functools.partial(backward_kernel, plan, per_device, lengths),
        in_specs=[smem, smem, vmem, hbm] + [hbm] * len(pieces),
        out_specs=pl.BlockSpec(memory_space=pltpu.VMEM),
        scratch_shapes=[
            pltpu.VMEM(vals.shape, BF16),
            pltpu.VMEM((sum(lengths), width, size), BF16),
            pltpu.VMEM((cols + 1, width, size), F32),
            pltpu.VMEM((2, slots), jnp.int32),
            pltpu.SMEM((2, slots), jnp.int32),
            pltpu.SemaphoreType.DMA((slots // GROUP,)),
            pltpu.SemaphoreType.DMA((len(pieces) + 1,)),
        ],
        out_shape=jax.ShapeDtypeStruct((cols, size, width), kind),
        compiler_params=pltpu.CompilerParams(vmem_limit_bytes=VMEM_LIMIT),
        cost_estimate=pl.CostEstimate(
            flops=8 * slots * size * size * width, bytes_accessed=4 * vals.size, transcendentals=0
        ),
        name="backward_blocks",
    )(live, me, coords, vals, *pieces)


def dense_kernel(first, *refs):
    terms_a, terms_b, (cot, weight, bias, out, grad_a, grad_b, terms) = refs[:4], refs[4:8], refs[8:]
    half = weight.shape[0] // 2
    size = grad_a.shape[2]
    at_a = pl.multiple_of(first[0] * half, half)
    at_b = pl.multiple_of((1 - first[0]) * half, half)

    def total(keep_0, got_0, keep_1, got_1):
        add_up = lambda x, y: (x[...].astype(F32) + y[...].astype(F32)).astype(BF16).reshape(-1, half)
        return jnp.concatenate([add_up(keep_0, got_0), add_up(keep_1, got_1)])

    agg_a, agg_b = total(*terms_a), total(*terms_b)
    weight_a, weight_b = weight[pl.ds(at_a, half), :], weight[pl.ds(at_b, half), :]
    preact = jnp.dot(agg_a, weight_a, preferred_element_type=F32)
    preact += jnp.dot(agg_b, weight_b, preferred_element_type=F32)
    preact += bias[...]
    gate = jax.nn.sigmoid(preact)
    out[...] = (preact * gate).astype(BF16)
    slope = gate * (1.0 + preact * (1.0 - gate))
    grad_pre = (cot[...].astype(F32) * slope).astype(BF16)
    over_rows = (((0,), (0,)), ((), ()))
    over_outputs = (((1,), (1,)), ((), ()))
    turned_a = lax.dot_general(weight_a, grad_pre, over_outputs, preferred_element_type=F32).astype(BF16)
    turned_b = lax.dot_general(weight_b, grad_pre, over_outputs, preferred_element_type=F32).astype(BF16)
    for at in range(grad_a.shape[0]):
        grad_a[at] = turned_a[:, at * size : (at + 1) * size]
        grad_b[at] = turned_b[:, at * size : (at + 1) * size]
    terms[pl.ds(at_a, half), :] = lax.dot_general(agg_a, grad_pre, over_rows, preferred_element_type=F32)
    terms[pl.ds(at_b, half), :] = lax.dot_general(agg_b, grad_pre, over_rows, preferred_element_type=F32)
    sums = jnp.sum(grad_pre.astype(F32), axis=0, keepdims=True)
    terms[2 * half :, :] = jnp.broadcast_to(sums, (terms.shape[0] - 2 * half, sums.shape[1]))


def dense(first, terms_a, terms_b, cot, weight, bias):
    run, size, half = terms_b[0].shape
    rows, width = cot.shape
    vmem = pl.BlockSpec(memory_space=pltpu.VMEM)
    turned = jax.ShapeDtypeStruct((rows // size, half, size), BF16)
    return pl.pallas_call(
        dense_kernel,
        in_specs=[pl.BlockSpec(memory_space=pltpu.SMEM)] + [vmem] * 11,
        out_specs=[vmem] * 4,
        out_shape=[
            jax.ShapeDtypeStruct((rows, width), BF16),
            turned,
            turned,
            jax.ShapeDtypeStruct((2 * half + 32, width), F32),
        ],
        compiler_params=pltpu.CompilerParams(vmem_limit_bytes=VMEM_LIMIT),
        cost_estimate=pl.CostEstimate(
            flops=8 * rows * width * width, bytes_accessed=8 * rows * width, transcendentals=rows * width
        ),
        name="dense_layer",
    )(first, *terms_a, *terms_b, cot, weight, bias)


def swap(array, axis, bit):
    return lax.ppermute(array, axis, [(at, at ^ bit) for at in range(lax.axis_size(axis))])


def after(array, *others):
    return lax.optimization_barrier((array, *others))[0]


def add(x, y):
    return (x.astype(F32) + y.astype(F32)).astype(BF16)


def halves(keep, got):
    half = keep.shape[0] // 2
    send = add(keep[half:], got[half:])
    return add(keep[:half], got[:half]), send


class SumOverAll:
    def __init__(self, terms):
        self.terms = self.got = terms
        self.bits = [1 << k for k in range(1, lax.axis_size("col").bit_length() - 1)]
        self.row_bits = [1]
        if lax.axis_size("row") == 2:
            half = terms.shape[0] // 2
            self.mine = lax.axis_index("col") % 2
            self.part = lax.dynamic_slice_in_dim(terms, self.mine * half, half)
            self.got = swap(lax.dynamic_slice_in_dim(terms, (1 - self.mine) * half, half), "col", 1)

    def step(self, take=lambda got: got):
        if lax.axis_size("row") == 2 and self.bits:
            self.part = self.part + take(self.got)
            if self.row_bits:
                self.got = swap(self.part, "row", self.row_bits.pop())
            else:
                self.got = swap(self.part, "col", self.bits.pop(0))

    def finish(self):
        if lax.axis_size("row") != 2:
            return lax.psum(self.terms, ("row", "col"))
        while self.bits:
            self.step()
        part = self.part + self.got
        other = swap(part, "col", 1)
        first, second = jnp.where(self.mine == 0, part, other), jnp.where(self.mine == 0, other, part)
        return jnp.concatenate([first, second])


def on_device(features, block_values, block_coords, live_blocks, weight, bias, cotangent):
    vals, coords, live = block_values[0, 0], block_coords[0, 0], live_blocks[0]
    size = vals.shape[1]
    row_count, count = lax.axis_size("row"), lax.axis_size("col")
    me = lax.axis_index("col").reshape(1)
    width = weight.shape[0]
    half = width // 2
    per_device = cotangent.shape[0] // size
    cols = features.shape[0] // size
    order_0, order_1 = orders(count)

    if row_count == 2:
        first = lax.axis_index("row").reshape(1)
        feats_a, feats_b = features, swap(features, "row", 1)
    else:
        first = jnp.zeros((1,), jnp.int32)
        feats = lax.all_gather(features, "row", axis=1, tiled=True)
        feats_a, feats_b = feats[:, :half], feats[:, half:]

    def products(feats, plan):
        keep, send = forward_blocks(live, me, coords, vals, feats.reshape(cols, size, half), plan, per_device)
        return keep, send, swap(send, "col", 1)

    def core_sums(keep, got):
        part = keep.shape[0] // 2
        return halves(keep[:part], got[:part]), halves(keep[part:], got[part:])

    plan_a, plan_b = (order_0, order_0), (order_0, order_1)
    keep_a, send_a, got_a = products(feats_a, plan_a)
    keep_b, send_b, got_b = products(after(feats_b, send_a), plan_b)
    parts = [*core_sums(keep_a, after(got_a, send_b)), *core_sums(keep_b, got_b)]
    plans = [*plan_a, *plan_b]
    taken, got = [got_b], {}

    def take(got):
        taken[0] = after(got, taken[0])
        return taken[0]

    steps = len(order_0) - 1
    turns = [(1, 0), (1, 3), (1, 1), (2, 0), (2, 1)]
    turns += [(step, part) for step in range(3, steps) for part in (0, 1)]
    turns += [(steps, 0), (1, 2), (2, 3), (2, 2), (steps, 1)]
    turns += [(step, part) for step in range(3, steps) for part in (3, 2)]
    turns += [(steps, 3), (steps, 2)]
    sent = {part: swap(parts[part][1], "col", plans[part][1]) for part in range(4)}
    for step, part in turns:
        sent[part] = take(sent[part])
        if step < steps:
            parts[part] = halves(parts[part][0], sent[part])
            sent[part] = swap(parts[part][1], "col", plans[part][step + 1])
    terms = []
    for part in range(4):
        terms += [parts[part][0], sent[part]]
    terms_a, terms_b = terms[:4], terms[4:]
    out, grad_a, grad_b, terms = dense(first, terms_a, terms_b, cotangent, weight, bias.reshape(1, -1))
    run = per_device // PARTS

    def input_grad(pieces, plan, kind):
        result = backward_blocks(live, me, coords, vals, pieces, cols, kind, plan, per_device)
        return result.reshape(-1, half)

    taken[0] = grad_b
    totals = SumOverAll(terms)
    outer, inner = list(reversed(order_0[2:])), order_0[1]
    steps_b = list(zip(reversed(order_0[1:-1]), reversed(order_1[1:-1])))
    cross = lambda piece: swap(piece, "col", inner)

    got_b = swap(grad_b, "col", outer[0])
    masks = [0]
    for bit in outer:
        masks = masks + [mask ^ bit for mask in masks]
    soon = [mask for mask in masks if not mask & outer[0]]
    pieces, crossed = {0: grad_a}, {0: cross(grad_a)}
    for mask in soon[1:]:
        pieces[mask] = swap(grad_a, "col", mask)
    crossed[0] = take(crossed[0])
    for mask in soon[1:]:
        pieces[mask] = take(pieces[mask])
        crossed[mask] = cross(pieces[mask])
    totals.step(take)
    got_b = take(got_b)
    for mask in masks:
        if mask not in pieces:
            pieces[mask] = swap(after(grad_a, got_b), "col", mask)
    parts_b = [jnp.concatenate([grad_b[at : at + run], got_b[at : at + run]]) for at in (0, run)]
    taken[0] = after(taken[0], *parts_b)
    late = [mask for mask in masks if mask not in soon]
    for at, bits in enumerate(steps_b):
        got = [swap(part, "col", bit) for part, bit in zip(parts_b, bits)]
        if at == 0:
            crossed.update({mask: take(crossed[mask]) for mask in soon[1:]})
        got[0] = take(got[0])
        if at == 1:
            core = {mask: [swap(piece[mask], "col", 1) for piece in (pieces, crossed)] for mask in soon}
            for mask in soon:
                core[mask] = [take(piece) for piece in core[mask]]
            totals.step(take)
        got[1] = take(got[1])
        parts_b = [jnp.concatenate([part, more]) for part, more in zip(parts_b, got)]
        taken[0] = after(taken[0], *parts_b)
        totals.step(take)
        if at == 0:
            for mask in late:
                pieces[mask] = take(pieces[mask])
                crossed[mask] = cross(pieces[mask])
    core_b = [take(swap(part, "col", 1)) for part in parts_b]
    pieces_b = [after(parts_b[0], *taken), core_b[0], parts_b[1], core_b[1]]

    part_b = input_grad(pieces_b, (order_0, order_1), BF16 if row_count == 2 else F32)
    for mask in late:
        crossed[mask] = after(crossed[mask], part_b)
        core[mask] = [swap(piece[mask], "col", 1) for piece in (pieces, crossed)]
    pieces_a = [pieces[mask] for mask in masks] + [crossed[mask] for mask in masks]
    pieces_a = pieces_a + [core[mask][0] for mask in masks] + [core[mask][1] for mask in masks]
    part_a = input_grad(pieces_a, (order_0,), F32)
    if row_count == 2:
        theirs = swap(part_b, "row", 1)
        grad_x = (part_a + theirs.astype(F32)).astype(BF16)
    else:
        partial_x = jnp.concatenate([part_a, part_b], axis=1)
        grad_x = lax.psum_scatter(partial_x, "row", scatter_dimension=1, tiled=True).astype(BF16)
    totals.got = after(totals.got, part_b)
    sums = totals.finish() * (cols * size * count) ** (-0.5)
    return out, grad_x, sums[:width], sums[width]


def solution(mesh):
    in_specs = (
        P("col", "row"),
        P("row", "col", None, None, None),
        P("row", "col", None, None),
        P("row", "col"),
        P(),
        P(),
        P(("row", "col"), None),
    )
    out_specs = (P(("row", "col"), None), P("col", "row"), P(), P())
    return jax.shard_map(
        on_device, mesh=mesh, in_specs=in_specs, out_specs=out_specs, check_vma=False
    )
```

```python
import functools
import math

import jax
import jax.numpy as jnp
from jax import lax
from jax.experimental import pallas as pl
from jax.experimental.pallas import tpu as pltpu
from jax.sharding import PartitionSpec as P

BF16 = jnp.bfloat16
F32 = jnp.float32
GROUP = 32
EARLY = 2
PARTS = 2
VMEM_LIMIT = 56 * 1024 * 1024


def orders(count):
    bits = [1 << k for k in range(count.bit_length() - 1)]
    swapped = list(bits)
    swapped[1], swapped[2] = bits[2], bits[1]
    return bits, swapped


def spot_of(apart, order):
    spot = apart * 0
    for k, bit in enumerate(reversed(order)):
        spot = spot + jnp.where((apart & bit) != 0, 1 << k, 0)
    return spot


def split_row(row, me, per_device, plan):
    run = per_device // len(plan)
    apart, at = (row // per_device) ^ me, row % per_device
    part = at // run
    spot = spot_of(apart, plan[0])
    for number, order in enumerate(plan[1:], 1):
        spot = jnp.where(part == number, spot_of(apart, order), spot)
    return spot, part, at % run


def clear(totals, count):
    steps = math.gcd(count, 16)
    height = count // steps

    def one(at, _):
        totals[pl.ds(at * height, height)] = jnp.zeros((height,) + totals.shape[1:], F32)
        return 0

    lax.fori_loop(0, steps, one, 0)


def start_table(sources, targets, table, scalars, sem):
    table[0:1, :] = sources
    table[1:2, :] = targets
    copy = pltpu.make_async_copy(table, scalars, sem)
    copy.start()
    return copy


def alive_slots(live, slots):
    return lax.broadcasted_iota(jnp.int32, (1, slots), 1) < live[0]


def block_copies(vals, held, sems):
    groups = held.shape[0] // GROUP
    part = lambda at: pl.ds(at * GROUP, GROUP)
    return [pltpu.make_async_copy(vals.at[part(at)], held.at[part(at)], sems.at[at]) for at in range(groups)]


def over_blocks(live, copies, body):
    for at, copy in enumerate(copies):

        @pl.when(at * GROUP < live[0])
        def _(at=at, copy=copy):
            copy.wait()
            for u in range(GROUP):
                body(at * GROUP + u)


def start_blocks(live, copies, first=0, last=None):
    for at, copy in list(enumerate(copies))[first:last]:

        @pl.when(at * GROUP < live[0])
        def _(copy=copy):
            copy.start()


def forward_kernel(
    plan, per_device, live, me, coords, vals, feats, keep, send, held, totals, rounded, table, scalars, sems, out_sems
):
    parts = len(plan)
    half, run = keep.shape[0], per_device // parts
    rows, below = 2 * half, half // per_device
    copies = block_copies(vals, held, sems)
    start_blocks(live, copies)
    spot, part, at = split_row(coords[0:1, :], me[0], per_device, plan)
    to = (((spot // below) * parts + part) * below + spot % below) * run + at
    to = jnp.where(alive_slots(live, to.shape[1]), to, rows)
    filled = start_table(coords[1:2, :], to, table, scalars, out_sems.at[0])
    clear(totals, rows)
    filled.wait()

    def one_slot(slot):
        to = scalars[1, slot]
        totals[to] += jnp.dot(held[slot], feats[scalars[0, slot]], preferred_element_type=F32)

    over_blocks(live, copies, one_slot)
    outs = []
    for at, out in ((1, send), (0, keep)):

        height = math.gcd(half, 8)

        def write(k, _, at=at):
            here = pl.ds(at * half + k * height, height)
            rounded[here] = totals[here].astype(BF16)
            return 0

        lax.fori_loop(0, half // height, write, 0)
        outs.append(pltpu.make_async_copy(rounded.at[pl.ds(at * half, half)], out, out_sems.at[at]))
        outs[-1].start()
    for out in outs:
        out.wait()


def forward_blocks(live, me, coords, vals, feats, plan, per_device):
    slots, size = vals.shape[0], vals.shape[1]
    width = feats.shape[2]
    rows = (1 << len(plan[0])) * per_device
    part = jax.ShapeDtypeStruct((rows // 2, size, width), BF16)
    smem, hbm = pl.BlockSpec(memory_space=pltpu.SMEM), pl.BlockSpec(memory_space=pl.ANY)
    vmem = pl.BlockSpec(memory_space=pltpu.VMEM)
    return pl.pallas_call(
        functools.partial(forward_kernel, plan, per_device),
        in_specs=[smem, smem, vmem, hbm, vmem],
        out_specs=[hbm, hbm],
        scratch_shapes=[
            pltpu.VMEM(vals.shape, BF16),
            pltpu.VMEM((rows + 1, size, width), F32),
            pltpu.VMEM((rows, size, width), BF16),
            pltpu.VMEM((2, slots), jnp.int32),
            pltpu.SMEM((2, slots), jnp.int32),
            pltpu.SemaphoreType.DMA((slots // GROUP,)),
            pltpu.SemaphoreType.DMA((2,)),
        ],
        out_shape=[part, part],
        compiler_params=pltpu.CompilerParams(vmem_limit_bytes=VMEM_LIMIT),
        cost_estimate=pl.CostEstimate(
            flops=8 * slots * size * size * width, bytes_accessed=4 * vals.size, transcendentals=0
        ),
        name="forward_blocks",
    )(live, me, coords, vals, feats)


def backward_kernel(plan, per_device, lengths, live, me, coords, vals, *refs):
    pieces, (out, held, grads, totals, table, scalars, sems, piece_sems) = refs[:-8], refs[-8:]
    run, cols, count = per_device // len(plan), out.shape[0], 1 << len(plan[0])
    copies = block_copies(vals, held, sems)
    fetches, start = [], 0
    for at, (piece, length) in enumerate(zip(pieces, lengths)):
        fetches.append(pltpu.make_async_copy(piece, grads.at[pl.ds(start, length)], piece_sems.at[at]))
        fetches[-1].start()
        start += length
    start_blocks(live, copies, last=EARLY)
    spot, part, at = split_row(coords[0:1, :], me[0], per_device, plan)
    alive = alive_slots(live, spot.shape[1])
    to = jnp.where(alive, coords[1:2, :], cols)
    filled = start_table((part * count + spot) * run + at, to, table, scalars, piece_sems.at[len(pieces)])
    clear(totals, cols)
    filled.wait()
    for fetch in fetches:
        fetch.wait()
    start_blocks(live, copies, first=EARLY)

    def one_slot(slot):
        to = scalars[1, slot]
        totals[to] += jnp.dot(grads[scalars[0, slot]], held[slot], preferred_element_type=F32)

    over_blocks(live, copies, one_slot)

    def write(at, _):
        out[at] = totals[at].astype(out.dtype).T
        return 0

    lax.fori_loop(0, cols, write, 0)


def backward_blocks(live, me, coords, vals, pieces, cols, kind, plan, per_device):
    slots, size = vals.shape[0], vals.shape[1]
    width = pieces[0].shape[1]
    lengths = tuple(piece.shape[0] for piece in pieces)
    smem, hbm = pl.BlockSpec(memory_space=pltpu.SMEM), pl.BlockSpec(memory_space=pl.ANY)
    vmem = pl.BlockSpec(memory_space=pltpu.VMEM)
    return pl.pallas_call(
        functools.partial(backward_kernel, plan, per_device, lengths),
        in_specs=[smem, smem, vmem, hbm] + [hbm] * len(pieces),
        out_specs=pl.BlockSpec(memory_space=pltpu.VMEM),
        scratch_shapes=[
            pltpu.VMEM(vals.shape, BF16),
            pltpu.VMEM((sum(lengths), width, size), BF16),
            pltpu.VMEM((cols + 1, width, size), F32),
            pltpu.VMEM((2, slots), jnp.int32),
            pltpu.SMEM((2, slots), jnp.int32),
            pltpu.SemaphoreType.DMA((slots // GROUP,)),
            pltpu.SemaphoreType.DMA((len(pieces) + 1,)),
        ],
        out_shape=jax.ShapeDtypeStruct((cols, size, width), kind),
        compiler_params=pltpu.CompilerParams(vmem_limit_bytes=VMEM_LIMIT),
        cost_estimate=pl.CostEstimate(
            flops=8 * slots * size * size * width, bytes_accessed=4 * vals.size, transcendentals=0
        ),
        name="backward_blocks",
    )(live, me, coords, vals, *pieces)


def dense_kernel(first, *refs):
    terms_a, terms_b, (cot, weight, bias, out, grad_a, grad_b, terms) = refs[:4], refs[4:8], refs[8:]
    half = weight.shape[0] // 2
    size = grad_a.shape[2]
    at_a = pl.multiple_of(first[0] * half, half)
    at_b = pl.multiple_of((1 - first[0]) * half, half)

    def total(keep_0, got_0, keep_1, got_1):
        add_up = lambda x, y: (x[...].astype(F32) + y[...].astype(F32)).astype(BF16).reshape(-1, half)
        return jnp.concatenate([add_up(keep_0, got_0), add_up(keep_1, got_1)])

    agg_a, agg_b = total(*terms_a), total(*terms_b)
    weight_a, weight_b = weight[pl.ds(at_a, half), :], weight[pl.ds(at_b, half), :]
    preact = jnp.dot(agg_a, weight_a, preferred_element_type=F32)
    preact += jnp.dot(agg_b, weight_b, preferred_element_type=F32)
    preact += bias[...]
    gate = jax.nn.sigmoid(preact)
    out[...] = (preact * gate).astype(BF16)
    slope = gate * (1.0 + preact * (1.0 - gate))
    grad_pre = (cot[...].astype(F32) * slope).astype(BF16)
    over_rows = (((0,), (0,)), ((), ()))
    over_outputs = (((1,), (1,)), ((), ()))
    turned_a = lax.dot_general(weight_a, grad_pre, over_outputs, preferred_element_type=F32).astype(BF16)
    turned_b = lax.dot_general(weight_b, grad_pre, over_outputs, preferred_element_type=F32).astype(BF16)
    for at in range(grad_a.shape[0]):
        grad_a[at] = turned_a[:, at * size : (at + 1) * size]
        grad_b[at] = turned_b[:, at * size : (at + 1) * size]
    terms[pl.ds(at_a, half), :] = lax.dot_general(agg_a, grad_pre, over_rows, preferred_element_type=F32)
    terms[pl.ds(at_b, half), :] = lax.dot_general(agg_b, grad_pre, over_rows, preferred_element_type=F32)
    sums = jnp.sum(grad_pre.astype(F32), axis=0, keepdims=True)
    terms[2 * half :, :] = jnp.broadcast_to(sums, (terms.shape[0] - 2 * half, sums.shape[1]))


def dense(first, terms_a, terms_b, cot, weight, bias):
    run, size, half = terms_b[0].shape
    rows, width = cot.shape
    vmem = pl.BlockSpec(memory_space=pltpu.VMEM)
    turned = jax.ShapeDtypeStruct((rows // size, half, size), BF16)
    return pl.pallas_call(
        dense_kernel,
        in_specs=[pl.BlockSpec(memory_space=pltpu.SMEM)] + [vmem] * 11,
        out_specs=[vmem] * 4,
        out_shape=[
            jax.ShapeDtypeStruct((rows, width), BF16),
            turned,
            turned,
            jax.ShapeDtypeStruct((2 * half + 32, width), F32),
        ],
        compiler_params=pltpu.CompilerParams(vmem_limit_bytes=VMEM_LIMIT),
        cost_estimate=pl.CostEstimate(
            flops=8 * rows * width * width, bytes_accessed=8 * rows * width, transcendentals=rows * width
        ),
        name="dense_layer",
    )(first, *terms_a, *terms_b, cot, weight, bias)


def swap(array, axis, bit):
    return lax.ppermute(array, axis, [(at, at ^ bit) for at in range(lax.axis_size(axis))])


def after(array, *others):
    return lax.optimization_barrier((array, *others))[0]


def add(x, y):
    return (x.astype(F32) + y.astype(F32)).astype(BF16)


def halves(keep, got):
    half = keep.shape[0] // 2
    send = add(keep[half:], got[half:])
    return add(keep[:half], got[:half]), send


class SumOverAll:
    def __init__(self, terms):
        self.terms = self.got = terms
        self.bits = [1 << k for k in range(1, lax.axis_size("col").bit_length() - 1)]
        self.row_bits = [1]
        if lax.axis_size("row") == 2:
            half = terms.shape[0] // 2
            self.mine = lax.axis_index("col") % 2
            self.part = lax.dynamic_slice_in_dim(terms, self.mine * half, half)
            self.got = swap(lax.dynamic_slice_in_dim(terms, (1 - self.mine) * half, half), "col", 1)

    def step(self, take=lambda got: got):
        if lax.axis_size("row") == 2 and self.bits:
            self.part = self.part + take(self.got)
            if self.row_bits:
                self.got = swap(self.part, "row", self.row_bits.pop())
            else:
                self.got = swap(self.part, "col", self.bits.pop(0))

    def finish(self):
        if lax.axis_size("row") != 2:
            return lax.psum(self.terms, ("row", "col"))
        while self.bits:
            self.step()
        part = self.part + self.got
        other = swap(part, "col", 1)
        first, second = jnp.where(self.mine == 0, part, other), jnp.where(self.mine == 0, other, part)
        return jnp.concatenate([first, second])


def on_device(features, block_values, block_coords, live_blocks, weight, bias, cotangent):
    vals, coords, live = block_values[0, 0], block_coords[0, 0], live_blocks[0]
    size = vals.shape[1]
    row_count, count = lax.axis_size("row"), lax.axis_size("col")
    me = lax.axis_index("col").reshape(1)
    width = weight.shape[0]
    half = width // 2
    per_device = cotangent.shape[0] // size
    cols = features.shape[0] // size
    order_0, order_1 = orders(count)

    if row_count == 2:
        first = lax.axis_index("row").reshape(1)
        feats_a, feats_b = features, swap(features, "row", 1)
    else:
        first = jnp.zeros((1,), jnp.int32)
        feats = lax.all_gather(features, "row", axis=1, tiled=True)
        feats_a, feats_b = feats[:, :half], feats[:, half:]

    def products(feats, plan):
        keep, send = forward_blocks(live, me, coords, vals, feats.reshape(cols, size, half), plan, per_device)
        return keep, send, swap(send, "col", 1)

    def core_sums(keep, got):
        part = keep.shape[0] // 2
        return halves(keep[:part], got[:part]), halves(keep[part:], got[part:])

    plan_a, plan_b = (order_0, order_0), (order_0, order_1)
    keep_a, send_a, got_a = products(feats_a, plan_a)
    keep_b, send_b, got_b = products(after(feats_b, send_a), plan_b)
    parts = [*core_sums(keep_a, after(got_a, send_b)), *core_sums(keep_b, got_b)]
    plans = [*plan_a, *plan_b]
    taken, got = [got_b], {}

    def take(got):
        taken[0] = after(got, taken[0])
        return taken[0]

    steps = len(order_0) - 1
    turns = [(1, 0), (1, 3), (1, 1), (2, 0), (2, 1)]
    turns += [(step, part) for step in range(3, steps) for part in (0, 1)]
    turns += [(steps, 0), (1, 2), (2, 3), (2, 2), (steps, 1)]
    turns += [(step, part) for step in range(3, steps) for part in (3, 2)]
    turns += [(steps, 3), (steps, 2)]
    sent = {part: swap(parts[part][1], "col", plans[part][1]) for part in range(4)}
    for step, part in turns:
        sent[part] = take(sent[part])
        if step < steps:
            parts[part] = halves(parts[part][0], sent[part])
            sent[part] = swap(parts[part][1], "col", plans[part][step + 1])
    terms = []
    for part in range(4):
        terms += [parts[part][0], sent[part]]
    terms_a, terms_b = terms[:4], terms[4:]
    out, grad_a, grad_b, terms = dense(first, terms_a, terms_b, cotangent, weight, bias.reshape(1, -1))
    run = per_device // PARTS

    def input_grad(pieces, plan, kind):
        result = backward_blocks(live, me, coords, vals, pieces, cols, kind, plan, per_device)
        return result.reshape(-1, half)

    taken[0] = grad_b
    totals = SumOverAll(terms)
    outer, inner = list(reversed(order_0[2:])), order_0[1]
    steps_b = list(zip(reversed(order_0[1:-1]), reversed(order_1[1:-1])))
    cross = lambda piece: swap(piece, "col", inner)

    got_b = swap(grad_b, "col", outer[0])
    masks = [0]
    for bit in outer:
        masks = masks + [mask ^ bit for mask in masks]
    soon = [mask for mask in masks if not mask & outer[0]]
    pieces, crossed = {0: grad_a}, {0: cross(grad_a)}
    for mask in soon[1:]:
        pieces[mask] = swap(grad_a, "col", mask)
    crossed[0] = take(crossed[0])
    for mask in soon[1:]:
        pieces[mask] = take(pieces[mask])
        crossed[mask] = cross(pieces[mask])
    totals.step(take)
    got_b = take(got_b)
    for mask in masks:
        if mask not in pieces:
            pieces[mask] = swap(after(grad_a, got_b), "col", mask)
    parts_b = [jnp.concatenate([grad_b[at : at + run], got_b[at : at + run]]) for at in (0, run)]
    taken[0] = after(taken[0], *parts_b)
    late = [mask for mask in masks if mask not in soon]
    for at, bits in enumerate(steps_b):
        got = [swap(part, "col", bit) for part, bit in zip(parts_b, bits)]
        if at == 0:
            crossed.update({mask: take(crossed[mask]) for mask in soon[1:]})
        got[0] = take(got[0])
        if at == 1:
            core = {mask: [swap(piece[mask], "col", 1) for piece in (pieces, crossed)] for mask in soon}
            for mask in soon:
                core[mask] = [take(piece) for piece in core[mask]]
            totals.step(take)
        got[1] = take(got[1])
        parts_b = [jnp.concatenate([part, more]) for part, more in zip(parts_b, got)]
        taken[0] = after(taken[0], *parts_b)
        if at == 0:
            totals.step(take)
            for mask in late:
                pieces[mask] = take(pieces[mask])
                crossed[mask] = cross(pieces[mask])
    core_b = [take(swap(part, "col", 1)) for part in parts_b]
    pieces_b = [after(parts_b[0], *taken), core_b[0], parts_b[1], core_b[1]]

    part_b = input_grad(pieces_b, (order_0, order_1), BF16 if row_count == 2 else F32)
    totals.got, part_b = lax.optimization_barrier((totals.got, part_b))
    totals.step()
    for mask in late:
        crossed[mask] = after(crossed[mask], part_b)
        core[mask] = [swap(piece[mask], "col", 1) for piece in (pieces, crossed)]
    pieces_a = [pieces[mask] for mask in masks] + [crossed[mask] for mask in masks]
    pieces_a = pieces_a + [core[mask][0] for mask in masks] + [core[mask][1] for mask in masks]
    part_a = input_grad(pieces_a, (order_0,), F32)
    totals.got, part_a = lax.optimization_barrier((totals.got, part_a))
    if row_count == 2:
        theirs = swap(part_b, "row", 1)
        grad_x = (part_a + theirs.astype(F32)).astype(BF16)
    else:
        partial_x = jnp.concatenate([part_a, part_b], axis=1)
        grad_x = lax.psum_scatter(partial_x, "row", scatter_dimension=1, tiled=True).astype(BF16)
    sums = totals.finish() * (cols * size * count) ** (-0.5)
    return out, grad_x, sums[:width], sums[width]


def solution(mesh):
    in_specs = (
        P("col", "row"),
        P("row", "col", None, None, None),
        P("row", "col", None, None),
        P("row", "col"),
        P(),
        P(),
        P(("row", "col"), None),
    )
    out_specs = (P(("row", "col"), None), P("col", "row"), P(), P())
    return jax.shard_map(
        on_device, mesh=mesh, in_specs=in_specs, out_specs=out_specs, check_vma=False
    )
```

```python
import functools
import math

import jax
import jax.numpy as jnp
from jax import lax
from jax.experimental import pallas as pl
from jax.experimental.pallas import tpu as pltpu
from jax.sharding import PartitionSpec as P

BF16 = jnp.bfloat16
F32 = jnp.float32
GROUP = 32
EARLY = 2
PARTS = 2
VMEM_LIMIT = 56 * 1024 * 1024


def orders(count):
    bits = [1 << k for k in range(count.bit_length() - 1)]
    swapped = list(bits)
    swapped[1], swapped[2] = bits[2], bits[1]
    return bits, swapped


def spot_of(apart, order):
    spot = apart * 0
    for k, bit in enumerate(reversed(order)):
        spot = spot + jnp.where((apart & bit) != 0, 1 << k, 0)
    return spot


def split_row(row, me, per_device, plan):
    run = per_device // len(plan)
    apart, at = (row // per_device) ^ me, row % per_device
    part = at // run
    spot = spot_of(apart, plan[0])
    for number, order in enumerate(plan[1:], 1):
        spot = jnp.where(part == number, spot_of(apart, order), spot)
    return spot, part, at % run


def clear(totals, count):
    steps = math.gcd(count, 16)
    height = count // steps

    def one(at, _):
        totals[pl.ds(at * height, height)] = jnp.zeros((height,) + totals.shape[1:], F32)
        return 0

    lax.fori_loop(0, steps, one, 0)


def start_table(sources, targets, table, scalars, sem):
    table[0:1, :] = sources
    table[1:2, :] = targets
    copy = pltpu.make_async_copy(table, scalars, sem)
    copy.start()
    return copy


def alive_slots(live, slots):
    return lax.broadcasted_iota(jnp.int32, (1, slots), 1) < live[0]


def block_copies(vals, held, sems):
    groups = held.shape[0] // GROUP
    part = lambda at: pl.ds(at * GROUP, GROUP)
    return [pltpu.make_async_copy(vals.at[part(at)], held.at[part(at)], sems.at[at]) for at in range(groups)]


def over_blocks(live, copies, body):
    for at, copy in enumerate(copies):

        @pl.when(at * GROUP < live[0])
        def _(at=at, copy=copy):
            copy.wait()
            for u in range(GROUP):
                body(at * GROUP + u)


def start_blocks(live, copies, first=0, last=None):
    for at, copy in list(enumerate(copies))[first:last]:

        @pl.when(at * GROUP < live[0])
        def _(copy=copy):
            copy.start()


def forward_kernel(
    plan, per_device, live, me, coords, vals, feats, keep, send, held, totals, rounded, table, scalars, sems, out_sems
):
    parts = len(plan)
    half, run = keep.shape[0], per_device // parts
    rows, below = 2 * half, half // per_device
    copies = block_copies(vals, held, sems)
    start_blocks(live, copies)
    spot, part, at = split_row(coords[0:1, :], me[0], per_device, plan)
    to = (((spot // below) * parts + part) * below + spot % below) * run + at
    to = jnp.where(alive_slots(live, to.shape[1]), to, rows)
    filled = start_table(coords[1:2, :], to, table, scalars, out_sems.at[0])
    clear(totals, rows)
    filled.wait()

    def one_slot(slot):
        to = scalars[1, slot]
        totals[to] += jnp.dot(held[slot], feats[scalars[0, slot]], preferred_element_type=F32)

    over_blocks(live, copies, one_slot)
    outs = []
    for at, out in ((1, send), (0, keep)):

        height = math.gcd(half, 8)

        def write(k, _, at=at):
            here = pl.ds(at * half + k * height, height)
            rounded[here] = totals[here].astype(BF16)
            return 0

        lax.fori_loop(0, half // height, write, 0)
        outs.append(pltpu.make_async_copy(rounded.at[pl.ds(at * half, half)], out, out_sems.at[at]))
        outs[-1].start()
    for out in outs:
        out.wait()


def forward_blocks(live, me, coords, vals, feats, plan, per_device):
    slots, size = vals.shape[0], vals.shape[1]
    width = feats.shape[2]
    rows = (1 << len(plan[0])) * per_device
    part = jax.ShapeDtypeStruct((rows // 2, size, width), BF16)
    smem, hbm = pl.BlockSpec(memory_space=pltpu.SMEM), pl.BlockSpec(memory_space=pl.ANY)
    vmem = pl.BlockSpec(memory_space=pltpu.VMEM)
    return pl.pallas_call(
        functools.partial(forward_kernel, plan, per_device),
        in_specs=[smem, smem, vmem, hbm, vmem],
        out_specs=[hbm, hbm],
        scratch_shapes=[
            pltpu.VMEM(vals.shape, BF16),
            pltpu.VMEM((rows + 1, size, width), F32),
            pltpu.VMEM((rows, size, width), BF16),
            pltpu.VMEM((2, slots), jnp.int32),
            pltpu.SMEM((2, slots), jnp.int32),
            pltpu.SemaphoreType.DMA((slots // GROUP,)),
            pltpu.SemaphoreType.DMA((2,)),
        ],
        out_shape=[part, part],
        compiler_params=pltpu.CompilerParams(vmem_limit_bytes=VMEM_LIMIT),
        cost_estimate=pl.CostEstimate(
            flops=8 * slots * size * size * width, bytes_accessed=4 * vals.size, transcendentals=0
        ),
        name="forward_blocks",
    )(live, me, coords, vals, feats)


def backward_kernel(plan, per_device, lengths, live, me, coords, vals, *refs):
    pieces, (out, held, grads, totals, table, scalars, sems, piece_sems) = refs[:-8], refs[-8:]
    run, cols, count = per_device // len(plan), out.shape[0], 1 << len(plan[0])
    copies = block_copies(vals, held, sems)
    fetches, start = [], 0
    for at, (piece, length) in enumerate(zip(pieces, lengths)):
        fetches.append(pltpu.make_async_copy(piece, grads.at[pl.ds(start, length)], piece_sems.at[at]))
        fetches[-1].start()
        start += length
    start_blocks(live, copies, last=EARLY)
    spot, part, at = split_row(coords[0:1, :], me[0], per_device, plan)
    alive = alive_slots(live, spot.shape[1])
    to = jnp.where(alive, coords[1:2, :], cols)
    filled = start_table((part * count + spot) * run + at, to, table, scalars, piece_sems.at[len(pieces)])
    clear(totals, cols)
    filled.wait()
    for fetch in fetches:
        fetch.wait()
    start_blocks(live, copies, first=EARLY)

    def one_slot(slot):
        to = scalars[1, slot]
        totals[to] += jnp.dot(grads[scalars[0, slot]], held[slot], preferred_element_type=F32)

    over_blocks(live, copies, one_slot)

    def write(at, _):
        out[at] = totals[at].astype(out.dtype).T
        return 0

    lax.fori_loop(0, cols, write, 0)


def backward_blocks(live, me, coords, vals, pieces, cols, kind, plan, per_device):
    slots, size = vals.shape[0], vals.shape[1]
    width = pieces[0].shape[1]
    lengths = tuple(piece.shape[0] for piece in pieces)
    smem, hbm = pl.BlockSpec(memory_space=pltpu.SMEM), pl.BlockSpec(memory_space=pl.ANY)
    vmem = pl.BlockSpec(memory_space=pltpu.VMEM)
    return pl.pallas_call(
        functools.partial(backward_kernel, plan, per_device, lengths),
        in_specs=[smem, smem, vmem, hbm] + [hbm] * len(pieces),
        out_specs=pl.BlockSpec(memory_space=pltpu.VMEM),
        scratch_shapes=[
            pltpu.VMEM(vals.shape, BF16),
            pltpu.VMEM((sum(lengths), width, size), BF16),
            pltpu.VMEM((cols + 1, width, size), F32),
            pltpu.VMEM((2, slots), jnp.int32),
            pltpu.SMEM((2, slots), jnp.int32),
            pltpu.SemaphoreType.DMA((slots // GROUP,)),
            pltpu.SemaphoreType.DMA((len(pieces) + 1,)),
        ],
        out_shape=jax.ShapeDtypeStruct((cols, size, width), kind),
        compiler_params=pltpu.CompilerParams(vmem_limit_bytes=VMEM_LIMIT),
        cost_estimate=pl.CostEstimate(
            flops=8 * slots * size * size * width, bytes_accessed=4 * vals.size, transcendentals=0
        ),
        name="backward_blocks",
    )(live, me, coords, vals, *pieces)


def dense_kernel(first, *refs):
    terms_a, terms_b, (cot, weight, bias, out, grad_a, grad_b, terms) = refs[:4], refs[4:8], refs[8:]
    half = weight.shape[0] // 2
    size = grad_a.shape[2]
    at_a = pl.multiple_of(first[0] * half, half)
    at_b = pl.multiple_of((1 - first[0]) * half, half)

    def total(keep_0, got_0, keep_1, got_1):
        add_up = lambda x, y: (x[...].astype(F32) + y[...].astype(F32)).astype(BF16).reshape(-1, half)
        return jnp.concatenate([add_up(keep_0, got_0), add_up(keep_1, got_1)])

    agg_a, agg_b = total(*terms_a), total(*terms_b)
    weight_a, weight_b = weight[pl.ds(at_a, half), :], weight[pl.ds(at_b, half), :]
    preact = jnp.dot(agg_a, weight_a, preferred_element_type=F32)
    preact += jnp.dot(agg_b, weight_b, preferred_element_type=F32)
    preact += bias[...]
    gate = jax.nn.sigmoid(preact)
    out[...] = (preact * gate).astype(BF16)
    slope = gate * (1.0 + preact * (1.0 - gate))
    grad_pre = (cot[...].astype(F32) * slope).astype(BF16)
    over_rows = (((0,), (0,)), ((), ()))
    over_outputs = (((1,), (1,)), ((), ()))
    turned_a = lax.dot_general(weight_a, grad_pre, over_outputs, preferred_element_type=F32).astype(BF16)
    turned_b = lax.dot_general(weight_b, grad_pre, over_outputs, preferred_element_type=F32).astype(BF16)
    for at in range(grad_a.shape[0]):
        grad_a[at] = turned_a[:, at * size : (at + 1) * size]
        grad_b[at] = turned_b[:, at * size : (at + 1) * size]
    terms[pl.ds(at_a, half), :] = lax.dot_general(agg_a, grad_pre, over_rows, preferred_element_type=F32)
    terms[pl.ds(at_b, half), :] = lax.dot_general(agg_b, grad_pre, over_rows, preferred_element_type=F32)
    sums = jnp.sum(grad_pre.astype(F32), axis=0, keepdims=True)
    terms[2 * half :, :] = jnp.broadcast_to(sums, (terms.shape[0] - 2 * half, sums.shape[1]))


def dense(first, terms_a, terms_b, cot, weight, bias):
    run, size, half = terms_b[0].shape
    rows, width = cot.shape
    vmem = pl.BlockSpec(memory_space=pltpu.VMEM)
    turned = jax.ShapeDtypeStruct((rows // size, half, size), BF16)
    return pl.pallas_call(
        dense_kernel,
        in_specs=[pl.BlockSpec(memory_space=pltpu.SMEM)] + [vmem] * 11,
        out_specs=[vmem] * 4,
        out_shape=[
            jax.ShapeDtypeStruct((rows, width), BF16),
            turned,
            turned,
            jax.ShapeDtypeStruct((2 * half + 32, width), F32),
        ],
        compiler_params=pltpu.CompilerParams(vmem_limit_bytes=VMEM_LIMIT),
        cost_estimate=pl.CostEstimate(
            flops=8 * rows * width * width, bytes_accessed=8 * rows * width, transcendentals=rows * width
        ),
        name="dense_layer",
    )(first, *terms_a, *terms_b, cot, weight, bias)


def swap(array, axis, bit):
    return lax.ppermute(array, axis, [(at, at ^ bit) for at in range(lax.axis_size(axis))])


def after(array, *others):
    return lax.optimization_barrier((array, *others))[0]


def add(x, y):
    return (x.astype(F32) + y.astype(F32)).astype(BF16)


def halves(keep, got):
    half = keep.shape[0] // 2
    send = add(keep[half:], got[half:])
    return add(keep[:half], got[:half]), send


class SumOverAll:
    def __init__(self, terms):
        self.terms = self.got = terms
        self.bits = [1 << k for k in range(1, lax.axis_size("col").bit_length() - 1)]
        self.row_bits = [1]
        if lax.axis_size("row") == 2:
            half = terms.shape[0] // 2
            self.mine = lax.axis_index("col") % 2
            self.part = lax.dynamic_slice_in_dim(terms, self.mine * half, half)
            self.got = swap(lax.dynamic_slice_in_dim(terms, (1 - self.mine) * half, half), "col", 1)

    def step(self, take=lambda got: got):
        if lax.axis_size("row") == 2 and self.bits:
            self.part = self.part + take(self.got)
            if self.row_bits:
                self.got = swap(self.part, "row", self.row_bits.pop())
            else:
                self.got = swap(self.part, "col", self.bits.pop(0))

    def finish(self):
        if lax.axis_size("row") != 2:
            return lax.psum(self.terms, ("row", "col"))
        while self.bits:
            self.step()
        part = self.part + self.got
        other = swap(part, "col", 1)
        first, second = jnp.where(self.mine == 0, part, other), jnp.where(self.mine == 0, other, part)
        return jnp.concatenate([first, second])


def on_device(features, block_values, block_coords, live_blocks, weight, bias, cotangent):
    vals, coords, live = block_values[0, 0], block_coords[0, 0], live_blocks[0]
    size = vals.shape[1]
    row_count, count = lax.axis_size("row"), lax.axis_size("col")
    me = lax.axis_index("col").reshape(1)
    width = weight.shape[0]
    half = width // 2
    per_device = cotangent.shape[0] // size
    cols = features.shape[0] // size
    order_0, order_1 = orders(count)

    if row_count == 2:
        first = lax.axis_index("row").reshape(1)
        feats_a, feats_b = features, swap(features, "row", 1)
    else:
        first = jnp.zeros((1,), jnp.int32)
        feats = lax.all_gather(features, "row", axis=1, tiled=True)
        feats_a, feats_b = feats[:, :half], feats[:, half:]

    def products(feats, plan):
        keep, send = forward_blocks(live, me, coords, vals, feats.reshape(cols, size, half), plan, per_device)
        return keep, send, swap(send, "col", 1)

    def core_sums(keep, got):
        part = keep.shape[0] // 2
        return halves(keep[:part], got[:part]), halves(keep[part:], got[part:])

    plan_a, plan_b = (order_0, order_0), (order_0, order_1)
    keep_a, send_a, got_a = products(feats_a, plan_a)
    keep_b, send_b, got_b = products(after(feats_b, send_a), plan_b)
    parts = [*core_sums(keep_a, after(got_a, send_b)), *core_sums(keep_b, got_b)]
    plans = [*plan_a, *plan_b]
    taken, got = [got_b], {}

    def take(got):
        taken[0] = after(got, taken[0])
        return taken[0]

    steps = len(order_0) - 1
    turns = [(1, 0), (1, 3), (1, 1), (2, 0), (2, 1)]
    turns += [(step, part) for step in range(3, steps) for part in (0, 1)]
    turns += [(steps, 0), (1, 2), (2, 3), (2, 2), (steps, 1)]
    turns += [(step, part) for step in range(3, steps) for part in (3, 2)]
    turns += [(steps, 3), (steps, 2)]
    sent = {part: swap(parts[part][1], "col", plans[part][1]) for part in range(4)}
    for step, part in turns:
        sent[part] = take(sent[part])
        if step < steps:
            parts[part] = halves(parts[part][0], sent[part])
            sent[part] = swap(parts[part][1], "col", plans[part][step + 1])
    terms = []
    for part in range(4):
        terms += [parts[part][0], sent[part]]
    terms_a, terms_b = terms[:4], terms[4:]
    out, grad_a, grad_b, terms = dense(first, terms_a, terms_b, cotangent, weight, bias.reshape(1, -1))
    run = per_device // PARTS

    def input_grad(pieces, plan, kind):
        result = backward_blocks(live, me, coords, vals, pieces, cols, kind, plan, per_device)
        return result.reshape(-1, half)

    taken[0] = grad_b
    totals = SumOverAll(terms)
    outer, inner = list(reversed(order_0[2:])), order_0[1]
    steps_b = list(zip(reversed(order_0[1:-1]), reversed(order_1[1:-1])))
    cross = lambda piece: swap(piece, "col", inner)

    got_b = swap(grad_b, "col", outer[0])
    masks = [0]
    for bit in outer:
        masks = masks + [mask ^ bit for mask in masks]
    soon = [mask for mask in masks if not mask & outer[0]]
    pieces, crossed = {0: grad_a}, {0: cross(grad_a)}
    for mask in soon[1:]:
        pieces[mask] = swap(grad_a, "col", mask)
    crossed[0] = take(crossed[0])
    for mask in soon[1:]:
        pieces[mask] = take(pieces[mask])
        crossed[mask] = cross(pieces[mask])
    totals.step(take)
    got_b = take(got_b)
    for mask in masks:
        if mask not in pieces:
            pieces[mask] = swap(after(grad_a, got_b), "col", mask)
    parts_b = [jnp.concatenate([grad_b[at : at + run], got_b[at : at + run]]) for at in (0, run)]
    taken[0] = after(taken[0], *parts_b)
    late = [mask for mask in masks if mask not in soon]
    for at, bits in enumerate(steps_b):
        got = [swap(part, "col", bit) for part, bit in zip(parts_b, bits)]
        if at == 0:
            crossed.update({mask: take(crossed[mask]) for mask in soon[1:]})
        got[0] = take(got[0])
        if at == 1:
            core = {mask: [swap(piece[mask], "col", 1) for piece in (pieces, crossed)] for mask in soon}
            for mask in soon:
                core[mask] = [take(piece) for piece in core[mask]]
            totals.step(take)
        got[1] = take(got[1])
        parts_b = [jnp.concatenate([part, more]) for part, more in zip(parts_b, got)]
        taken[0] = after(taken[0], *parts_b)
        if at == 0:
            totals.step(take)
            for mask in late:
                pieces[mask] = take(pieces[mask])
                crossed[mask] = cross(pieces[mask])
    core_b = [take(swap(part, "col", 1)) for part in parts_b]
    pieces_b = [after(parts_b[0], *taken), core_b[0], parts_b[1], core_b[1]]

    part_b = input_grad(pieces_b, (order_0, order_1), BF16 if row_count == 2 else F32)
    totals.got, part_b = lax.optimization_barrier((totals.got, part_b))
    totals.step()
    for mask in late:
        crossed[mask] = after(crossed[mask], part_b)
        core[mask] = [swap(piece[mask], "col", 1) for piece in (pieces, crossed)]
    pieces_a = [pieces[mask] for mask in masks] + [crossed[mask] for mask in masks]
    pieces_a = pieces_a + [core[mask][0] for mask in masks] + [core[mask][1] for mask in masks]
    part_a = input_grad(pieces_a, (order_0,), BF16 if row_count == 2 else F32)
    totals.got, part_a = lax.optimization_barrier((totals.got, part_a))
    if row_count == 2:
        theirs = swap(part_b, "row", 1)
        grad_x = add(part_a, theirs)
    else:
        partial_x = jnp.concatenate([part_a, part_b], axis=1)
        grad_x = lax.psum_scatter(partial_x, "row", scatter_dimension=1, tiled=True).astype(BF16)
    sums = totals.finish() * (cols * size * count) ** (-0.5)
    return out, grad_x, sums[:width], sums[width]


def solution(mesh):
    in_specs = (
        P("col", "row"),
        P("row", "col", None, None, None),
        P("row", "col", None, None),
        P("row", "col"),
        P(),
        P(),
        P(("row", "col"), None),
    )
    out_specs = (P(("row", "col"), None), P("col", "row"), P(), P())
    return jax.shard_map(
        on_device, mesh=mesh, in_specs=in_specs, out_specs=out_specs, check_vma=False
    )
```
